512 devices in a mesh: dp: 32 (over z, x_lo, core), tensor: 16 (over y, x_hi).
Axes of the slice: x: 4 (x_hi: 2, x_lo: 2; x = x_hi * 2 + x_lo), y: 8, z: 8, core: 2. Of those that a mesh axis runs over, the one named last changes fastest.
Arguments:
- queries: bfloat16 [32, 1792, 6144], P('dp', 'tensor'), may hold values from -100 to 100
- keys: bfloat16 [32, 1792, 1024], P('dp', 'tensor'), may hold values from -8 to 8
- values: bfloat16 [32, 1792, 1024], P('dp', 'tensor'), may hold values from -6 to 6
- out_grad: bfloat16 [32, 1792, 6144], P('dp', 'tensor'), may hold values from -6 to 6
- loss_mask: int32 [32, 1792], P('dp', 'tensor'), may hold values from 0 to 1, as said below
Outputs:
- query_grad: bfloat16 [32, 1792, 6144], P('dp', 'tensor')
- key_grad: bfloat16 [32, 1792, 1024], P('dp', 'tensor')
- value_grad: bfloat16 [32, 1792, 1024], P('dp', 'tensor')
The draws below stay inside these ranges and needn't reach their ends.
Inputs may be any that keep to these rules, and one draw needn't show every extreme that they name: `loss_mask`: the first token of every micro-batch is live.
All inputs are finite; a program needn't handle non-finite values.
Results may differ from the reference program's by a relative error of at most 0.01.
Values may be sent and summed in bfloat16 or wider, within the bound.
A program may use at most 64 MiB of HBM per device.

```python
import jax
import jax.numpy as jnp
from jax import lax

HD = 128
BATCH = 32
TOKENS = 1792
HEADS = 48
KVH = 8
SEQ_LEN = 1792


def shared_keys(key):
    return jax.random.normal(key, (BATCH, TOKENS, KVH, HD), jnp.float32)


def draw_keys(key, part):
    base = shared_keys(key)
    return base.reshape(BATCH, TOKENS, KVH * HD).astype(jnp.bfloat16)


def draw_queries(key, part):
    key = jax.random.fold_in(key, 3)
    group = HEADS // KVH
    fresh = jax.random.normal(key, (BATCH, TOKENS, KVH, group, HD), jnp.float32)
    return fresh.reshape(BATCH, TOKENS, HEADS * HD).astype(jnp.bfloat16)


def draw_loss_mask(key, part):
    key = jax.random.fold_in(key, 9)
    spread = max(BATCH - 1, 1)
    mode_pick = jax.random.randint(jax.random.fold_in(key, 1), (), 0, 2)
    upper_level = jax.random.randint(jax.random.fold_in(key, 2), (), 150, 181)
    lower_level = jax.random.randint(jax.random.fold_in(key, 3), (), 70, 101)
    common = jnp.where(mode_pick == 1, upper_level, lower_level)
    batch_index = jnp.arange(BATCH, dtype=jnp.int32)
    ramped = common * (2 * spread + 7 * batch_index) // (2 * spread)
    jitter = jax.random.randint(jax.random.fold_in(key, 4), (BATCH,), 80, 121)
    span_count = (TOKENS + 15) // 16
    profile = jax.random.randint(jax.random.fold_in(key, 5), (span_count,), 25, 101)
    span_index = jnp.arange(TOKENS, dtype=jnp.int32) // 16
    span_rate = profile[span_index]
    levels = (ramped * jitter)[:, None] * span_rate[None, :]
    random_rolls = jax.random.randint(jax.random.fold_in(key, 6), (BATCH, TOKENS), 0, 10000000)
    alive_now = random_rolls < levels
    first_token = jnp.arange(TOKENS, dtype=jnp.int32)[None, :] == 0
    return jnp.where(first_token, True, alive_now).astype(jnp.int32)


def steps_of(key, dims, split, smallest, high):
    gain, own = 1.0, jax.random.fold_in(key, 6)
    for axis_at, blocks in split:
        heights = jnp.exp(jax.random.uniform(jax.random.fold_in(own, axis_at), (blocks,), jnp.float32, smallest / len(split), high / len(split)))
        gain = gain * jnp.repeat(heights, dims[axis_at] // blocks).reshape([-1 if axis == axis_at else 1 for axis in range(len(dims))])
    return gain


def normal_values(rng, shape, scale, most, split=(), kind=jnp.bfloat16):
    drawn = jax.random.normal(rng, shape, jnp.float32) * scale
    if len(split) > 0:
        drawn = steps_of(rng, shape, split, -0.22, 0.18) * drawn
    return jnp.clip(drawn, min=-most, max=most).astype(kind)


def setup_inputs(seed: int = 0) -> dict:
    streams_of = jax.random.split(jax.random.key(seed), 6)
    return {
        "queries": draw_queries(jax.random.fold_in(streams_of[5], 71), 0),
        "keys": draw_keys(jax.random.fold_in(streams_of[5], 71), 0),
        "values": normal_values(streams_of[2], (BATCH, TOKENS, KVH * HD), 1.0, 6.0, ((0, 32), (1, 16))),
        "out_grad": normal_values(streams_of[3], (BATCH, TOKENS, HEADS * HD), 1.0, 6.0, ((0, 32), (1, 16))),
        "loss_mask": draw_loss_mask(jax.random.fold_in(streams_of[5], 71), 0),
    }


def sequence_grads(parts):
    query_part, key_part, value_part, grad_part = parts
    scale = HD ** -0.5
    qf = query_part.astype(jnp.float32)
    kf = key_part.astype(jnp.float32)
    vf = value_part.astype(jnp.float32)
    gf = grad_part.astype(jnp.float32)
    scores = jnp.einsum('ikphd,jkd->kphij', qf, kf) * scale
    places = jnp.arange(SEQ_LEN)
    causal = places[:, None] >= places[None, :]
    scores = jnp.where(causal, scores, jnp.float32(-1e30))
    top = jnp.max(scores, axis=-1, keepdims=True)
    probs = jnp.exp(scores - top)
    probs = probs / jnp.sum(probs, axis=-1, keepdims=True)
    probs_b = lax.optimization_barrier(probs.astype(jnp.bfloat16)).astype(jnp.float32)
    value_sum = jnp.einsum('kphij,ikphd->jkpd', probs_b, gf)
    dprob = jnp.einsum('ikphd,jkd->kphij', gf, vf)
    delta = jnp.sum(probs * dprob, axis=-1, keepdims=True)
    dscore = lax.optimization_barrier((probs * (dprob - delta)).astype(jnp.bfloat16)).astype(jnp.float32)
    query_sum = jnp.einsum('kphij,jkd->ikphd', dscore, kf) * scale
    key_sum = jnp.einsum('kphij,ikphd->jkpd', dscore, qf) * scale
    return query_sum, key_sum, value_sum


def reference(queries, keys, values, out_grad, loss_mask):
    seqs = TOKENS // SEQ_LEN
    half = HEADS // KVH // 2
    count = jnp.sum(loss_mask.astype(jnp.float32))
    factor = jnp.float32(BATCH * TOKENS) / count

    def one_batch(parts):
        qb, kb, vb, gb, mb = parts
        masked = gb * mb[:, None].astype(jnp.bfloat16)
        q6 = qb.reshape(seqs, SEQ_LEN, KVH, 2, half, HD)
        g6 = masked.reshape(seqs, SEQ_LEN, KVH, 2, half, HD)
        k4 = kb.reshape(seqs, SEQ_LEN, KVH, HD)
        v4 = vb.reshape(seqs, SEQ_LEN, KVH, HD)
        query_sum, key_sum, value_sum = lax.map(sequence_grads, (q6, k4, v4, g6))
        query_out = (query_sum * factor).astype(jnp.bfloat16).reshape(TOKENS, HEADS * HD)
        key_halves = lax.optimization_barrier((key_sum * factor).astype(jnp.bfloat16)).astype(jnp.float32)
        value_halves = lax.optimization_barrier((value_sum * factor).astype(jnp.bfloat16)).astype(jnp.float32)
        key_out = (key_halves[:, :, :, 0] + key_halves[:, :, :, 1]).astype(jnp.bfloat16).reshape(TOKENS, KVH * HD)
        value_out = (value_halves[:, :, :, 0] + value_halves[:, :, :, 1]).astype(jnp.bfloat16).reshape(TOKENS, KVH * HD)
        return query_out, key_out, value_out

    query_grad, key_grad, value_grad = lax.map(one_batch, (queries, keys, values, out_grad, loss_mask))
    return (query_grad, key_grad, value_grad)
```

```python
import jax
import jax.numpy as jnp
from jax import lax
from jax.experimental import pallas as pl
from jax.experimental.pallas import tpu as pltpu
from jax.sharding import PartitionSpec as P

HD = 128
KVH = 8
GROUP = 6
KVD = KVH // 2
RING = 8
UP = 4
DOWN = 3
SCALE = HD**-0.5
SCALE2 = SCALE * 1.4426950408889634
NT = (((1,), (1,)), ((), ()))
TN = (((0,), (0,)), ((), ()))
MESH = pl.DeviceIdType.MESH
f32 = jnp.float32
bf16 = jnp.bfloat16


def fold8(x):
    return x.reshape(x.shape[0] // 8, 8, x.shape[1])


def make_kernel(tok, dp_size, ways, block):
    rows2 = GROUP * tok
    rows = 2 * rows2
    pair = 2 * tok
    length = ways * tok
    blocks = length // block
    chunks = [(i, min(256, rows - i)) for i in range(0, rows, 256)]
    dp_bits = dp_size.bit_length() - 1
    t_bits = ways.bit_length() - 1

    def kernel(
        q_ref, k_ref, v_ref, g_ref, mask_ref, dq_ref, dk_ref, dv_ref,
        qg, kv, qg_out, kv_out, sbuf, pbuf, ebuf, dsb, dqt, qn, gn, stat, rowpos,
        part, rs_out, rs_in, dq_out, dq_in, dkv_out, dkv_in, cnt_out, cnt_in,
        x_send, x_recv, ag_send, ag_recv, rs_send, rs_recv, cnt_send, cnt_recv,
    ):
        me_dp = lax.axis_index("dp")
        me = lax.axis_index("tensor")
        side = lax.rem(me, 2)
        y = me // 2

        def flip(index, bit):
            step = 1 << bit
            return index + step * (1 - 2 * lax.rem(index // step, 2))

        other = (me_dp, flip(me, 0))
        above = (me_dp, lax.rem(me + 2, ways))
        below = (me_dp, lax.rem(me + ways - 2, ways))
        doubling = [(me_dp, flip(me, bit)) for bit in range(t_bits)] + [
            (flip(me_dp, bit), me) for bit in range(dp_bits)
        ]
        peers = [other, above, below] + doubling[2:]

        @pl.when(y < RING - 1)
        def _():
            after = pl.ds(pl.multiple_of((y + 1) * pair, 16), pair)
            for h in range(KVD):
                kv[h, :, after, :] = jnp.zeros((2, pair, HD), bf16)

        barrier = pltpu.get_barrier_semaphore()
        for peer in peers:
            pl.semaphore_signal(barrier, inc=1, device_id=peer, device_id_type=MESH)

        def remote(src, dst, send, recv, device):
            return pltpu.make_async_remote_copy(
                src_ref=src, dst_ref=dst, send_sem=send, recv_sem=recv,
                device_id=device, device_id_type=MESH,
            )

        mask_row = mask_ref[...].astype(f32)
        eye = lax.broadcasted_iota(jnp.int32, (tok, tok), 0) == lax.broadcasted_iota(
            jnp.int32, (tok, tok), 1
        )
        mask_col = jnp.sum(jnp.where(eye, mask_row, 0.0), axis=1, keepdims=True)
        mask_tile = jnp.broadcast_to(mask_col, (tok, HD)).astype(bf16)
        cnt_out[0] = jnp.full((8, 128), jnp.sum(mask_row, keepdims=True)[0:1, 0:1], f32)

        own_rows = pl.multiple_of(side * rows2, 16)
        own_tok = pl.multiple_of(y * pair + side * tok, 16)

        def stage(h, _):
            for p in range(GROUP):
                at = pl.ds(p * tok, tok)
                mine = pl.ds(pl.multiple_of(((side * KVD + h) * GROUP + p) * HD, HD), HD)
                theirs = pl.ds(pl.multiple_of((((1 - side) * KVD + h) * GROUP + p) * HD, HD), HD)
                keep = pl.ds(pl.multiple_of(own_rows + p * tok, 16), tok)
                qg[h, 0, keep, :] = q_ref[:, mine]
                qg[h, 1, keep, :] = g_ref[:, mine] * mask_tile
                qg_out[h, 0, at, :] = q_ref[:, theirs]
                qg_out[h, 1, at, :] = g_ref[:, theirs] * mask_tile
            mine = pl.ds(pl.multiple_of((side * KVD + h) * HD, HD), HD)
            theirs = pl.ds(pl.multiple_of(((1 - side) * KVD + h) * HD, HD), HD)
            kv[h, 0, pl.ds(own_tok, tok), :] = k_ref[:, mine]
            kv[h, 1, pl.ds(own_tok, tok), :] = v_ref[:, mine]
            kv_out[h, 0] = k_ref[:, theirs]
            kv_out[h, 1] = v_ref[:, theirs]
            return 0

        lax.fori_loop(0, KVD, stage, 0)
        index = lax.broadcasted_iota(jnp.int32, (8, rows), 1)
        place = index
        for step in range(1, 2 * GROUP):
            place = place - jnp.where(index >= step * tok, tok, 0)
        rowpos[...] = place + jnp.where(index >= rows2, tok, 0)

        pl.semaphore_wait(barrier, len(peers))

        def x_copy(kind, h):
            src, dst = {
                0: lambda: (kv_out.at[h], kv.at[h, :, pl.ds(own_tok, tok), :]),
                1: lambda: (qg_out.at[h], qg.at[h, :, pl.ds(own_rows, rows2), :]),
                2: lambda: (dq_out.at[h], dq_in.at[h]),
                3: lambda: (dkv_out.at[h], dkv_in.at[h]),
            }[kind]()
            return remote(src, dst, x_send.at[kind, h], x_recv.at[kind, h], other)

        def ag_copy(h, s, up):
            j = y - s if up else lax.rem(y + s, RING)
            span = pl.ds(pl.multiple_of(jnp.maximum(j, 0) * pair, 16), pair)
            place = kv.at[h, :, span, :]
            slot = s if up else UP + s
            return remote(
                place, place, ag_send.at[h, slot], ag_recv.at[h, slot], above if up else below
            )

        def ag_send_when(s, up):
            if up:
                return jnp.logical_and(y < RING - 1, y >= s)
            return lax.rem(y + s, RING) < DOWN

        def ag_recv_when(s, up):
            if up:
                return y >= s + 1
            return lax.rem(y + 1 + s, RING) < DOWN

        def ag_start(h, s):
            for up in (True, False):
                if s < (UP if up else DOWN):
                    pl.when(ag_send_when(s, up))(lambda up=up: ag_copy(h, s, up).start())

        def ag_wait(h, s):
            for up in (True, False):
                if s < (UP if up else DOWN):
                    pl.when(ag_recv_when(s, up))(lambda up=up: ag_copy(h, s, up).wait_recv())

        def rs_copy(h, s, down):
            slot = s if down else UP + s
            return remote(
                rs_out.at[h, slot], rs_in.at[h, slot], rs_send.at[h, slot], rs_recv.at[h, slot],
                below if down else above,
            )

        def rs_block(s, down):
            return y - UP + s if down else lax.rem(y + DOWN - s, RING)

        def rs_send_when(s, down):
            if down:
                return y >= UP - s
            return lax.rem(y + DOWN - s, RING) < DOWN

        def rs_recv_when(s, down):
            if down:
                return jnp.logical_and(y < RING - 1, y >= UP - 1 - s)
            return lax.rem(y + DOWN - 1 - s, RING) < DOWN

        def rs_take(h, s, down):
            pl.when(rs_recv_when(s, down))(lambda: rs_copy(h, s, down).wait_recv())

        def part_scaled(h, j):
            span = pl.ds(pl.multiple_of(jnp.maximum(j, 0) * pair, 16), pair)
            slot = lax.rem(h, 2)
            return [part[slot, i, span, :] for i in range(2)]

        def rs_start(h, s):
            for down in (True, False):
                if s >= (UP if down else DOWN):
                    continue
                if s > 0:
                    rs_take(h, s - 1, down)
                slot = s if down else UP + s
                j = rs_block(s, down)
                here = rs_send_when(s, down)
                if down:
                    first = jnp.logical_or(y == RING - 1, s == 0)
                    cases = [(True, False, first), (True, True, jnp.logical_not(first))]
                else:
                    owns = y > j
                    cases = [(True, s > 0, owns)] + (
                        [(False, True, jnp.logical_not(owns))] if s > 0 else []
                    )
                for mine, came, when in cases:
                    if down and came and s == 0:
                        continue

                    def fill(mine=mine, came=came, slot=slot, j=j, down=down):
                        values = part_scaled(h, j) if mine else None
                        for i in range(2):
                            if mine and came:
                                total = values[i] + rs_in[h, slot - 1, i].astype(f32)
                                rs_out[h, slot, i] = total.astype(bf16)
                            elif mine:
                                rs_out[h, slot, i] = values[i].astype(bf16)
                            else:
                                rs_out[h, slot, i] = rs_in[h, slot - 1, i]
                        rs_copy(h, s, down).start()

                    pl.when(jnp.logical_and(here, when))(fill)

        def rs_finish(h):
            rs_take(h, UP - 1, True)
            rs_take(h, DOWN - 1, False)
            slot = lax.rem(h, 2)
            mine_at = pl.ds(own_tok, tok)
            theirs_at = pl.ds(pl.multiple_of(y * pair + (1 - side) * tok, 16), tok)
            mine_in = pl.ds(pl.multiple_of(side * tok, 16), tok)
            theirs_in = pl.ds(pl.multiple_of((1 - side) * tok, 16), tok)
            columns = pl.ds(pl.multiple_of((side * KVD + h) * HD, HD), HD)
            from_above = y < RING - 1
            from_below = y < DOWN

            def total(i, at, within, above_too, below_too):
                value = part[slot, i, at, :]
                if above_too:
                    value = value + rs_in[h, UP - 1, i, within, :].astype(f32)
                if below_too:
                    value = value + rs_in[h, UP + DOWN - 1, i, within, :].astype(f32)
                return value.astype(bf16)

            for above_too, below_too, when in (
                (True, True, from_below),
                (True, False, jnp.logical_and(from_above, jnp.logical_not(from_below))),
                (False, False, jnp.logical_not(from_above)),
            ):

                def fill(above_too=above_too, below_too=below_too):
                    for i, ref in ((0, dk_ref), (1, dv_ref)):
                        dkv_out[h, i] = total(i, theirs_at, theirs_in, above_too, below_too)
                        ref[:, columns] = total(i, mine_at, mine_in, above_too, below_too)

                pl.when(when)(fill)
            x_copy(3, h).start()

        def count_copy(n):
            return remote(
                cnt_out.at[n], cnt_in.at[n], cnt_send.at[n], cnt_recv.at[n], doubling[n]
            )

        count_left = list(range(len(doubling)))

        def count_rounds(number):
            for _ in range(number):
                if not count_left:
                    return
                n = count_left.pop(0)
                copy = count_copy(n)
                copy.start()
                copy.wait_recv()
                cnt_out[n + 1] = cnt_out[n] + cnt_in[n]

        x_copy(0, 0).start()
        x_copy(1, 0).start()
        for h in range(1, KVD):
            x_copy(0, h).start()
        count_rounds(1)
        x_copy(0, 0).wait_recv()
        ag_start(0, 0)
        for s in range(1, UP):
            count_rounds(2)
            ag_wait(0, s - 1)
            ag_start(0, s)
        count_rounds(len(doubling))
        ag_wait(0, UP - 1)
        count = cnt_out[len(doubling)]
        factor = f32(dp_size * length) / count[0:1, :]

        full_blocks = (pair * y + 1) // block
        all_blocks = jnp.minimum(blocks, (pair * (y + 1) + block - 1) // block)

        def one_head(h, _):
            more = h + 1 < KVD
            before = h > 0
            x_copy(1, h).wait_recv()

            @pl.when(more)
            def _():
                x_copy(1, h + 1).start()
                x_copy(0, h + 1).wait_recv()
                ag_start(h + 1, 0)

            def between(s):
                pl.when(more)(lambda: (ag_wait(h + 1, s - 1), ag_start(h + 1, s))[0])
                pl.when(before)(lambda: rs_start(h - 1, s))

            stat[0] = jnp.full((8, rows), -1e30, f32)

            def scores(masked):
                def step(b, _):
                    at = pl.ds(pl.multiple_of(b * block, block), block)
                    key_block = kv[h, 0, at, :]
                    value_block = kv[h, 1, at, :]
                    for c0, cw in chunks:
                        cs = pl.ds(c0, cw)
                        s = lax.dot_general(
                            key_block, qg[h, 0, cs, :], NT, preferred_element_type=f32
                        )
                        if masked:
                            key_at = (
                                b * block - pair * y
                                + lax.broadcasted_iota(jnp.int32, (block, cw), 0)
                            )
                            s = jnp.where(key_at <= rowpos[0:1, cs], s, -1e30)
                        sbuf[at, cs] = s
                        stat[0, :, cs] = jnp.maximum(stat[0, :, cs], jnp.max(fold8(s), axis=0))
                        pbuf[at, cs] = lax.dot_general(
                            value_block, qg[h, 1, cs, :], NT, preferred_element_type=f32
                        )
                    return 0

                return step

            lax.fori_loop(0, full_blocks, scores(False), 0)
            lax.fori_loop(full_blocks, all_blocks, scores(True), 0)
            between(1)
            top = jnp.max(stat[0], axis=0, keepdims=True) * SCALE2
            stat[0] = jnp.broadcast_to(top, (8, rows))
            stat[1] = jnp.zeros((8, rows), f32)
            stat[2] = jnp.zeros((8, rows), f32)

            def weights(b, _):
                at = pl.ds(pl.multiple_of(b * block, block), block)
                for c0, cw in chunks:
                    cs = pl.ds(c0, cw)
                    e = jnp.exp2(sbuf[at, cs] * SCALE2 - stat[0, 0:1, cs])
                    ebuf[at, cs] = e.astype(bf16)
                    stat[1, :, cs] += jnp.sum(fold8(e), axis=0)
                    stat[2, :, cs] += jnp.sum(fold8(e * pbuf[at, cs]), axis=0)
                return 0

            lax.fori_loop(0, all_blocks, weights, 0)
            between(2)
            inverse = 1.0 / jnp.sum(stat[1], axis=0, keepdims=True)
            delta = jnp.sum(stat[2], axis=0, keepdims=True) * inverse
            stat[3] = jnp.broadcast_to(delta, (8, rows))
            inverse_column = jnp.transpose(jnp.broadcast_to(inverse, (8, rows)))[:, 0:1]
            qn[...] = (qg[h, 0].astype(f32) * inverse_column).astype(bf16)
            gn[...] = (qg[h, 1].astype(f32) * inverse_column).astype(bf16)
            dqt[...] = jnp.zeros((HD, rows), f32)
            slot = lax.rem(h, 2)

            def grads(b, _):
                at = pl.ds(pl.multiple_of(b * block, block), block)
                key_block = kv[h, 0, at, :]
                for c0, cw in chunks:
                    cs = pl.ds(c0, cw)
                    ds = ebuf[at, cs] * (pbuf[at, cs] - stat[3, 0:1, cs]).astype(bf16)
                    dsb[:, cs] = ds
                    dqt[:, cs] += lax.dot_general(key_block, ds, TN, preferred_element_type=f32)
                part[slot, 1, at, :] = factor * jnp.dot(
                    ebuf[at, :], gn[...], preferred_element_type=f32
                )
                part[slot, 0, at, :] = (factor * SCALE) * jnp.dot(
                    dsb[...], qn[...], preferred_element_type=f32
                )
                return 0

            lax.fori_loop(0, all_blocks, grads, 0)
            between(3)
            rs_start(h, 0)
            stat[0] = jnp.broadcast_to(inverse * (factor[:, 0:1] * SCALE), (8, rows))
            dqt[...] = dqt[...] * stat[0, 0:1, :]
            dq_rows = jnp.transpose(dqt[...]).astype(bf16)

            def hand_out(mine, theirs):
                dq_out[h] = theirs
                for p in range(GROUP):
                    column = pl.multiple_of(((side * KVD + h) * GROUP + p) * HD, HD)
                    dq_ref[:, pl.ds(column, HD)] = mine[p * tok : (p + 1) * tok]

            pl.when(side == 0)(lambda: hand_out(dq_rows[:rows2], dq_rows[rows2:]))
            pl.when(side == 1)(lambda: hand_out(dq_rows[rows2:], dq_rows[:rows2]))
            x_copy(2, h).start()
            pl.when(more)(lambda: ag_wait(h + 1, UP - 1))
            pl.when(before)(lambda: rs_finish(h - 1))
            return 0

        lax.fori_loop(0, KVD, one_head, 0)
        last = KVD - 1
        for s in range(1, UP):
            rs_start(last, s)
        rs_finish(last)

        def collect(h, _):
            x_copy(2, h).wait_recv()
            for p in range(GROUP):
                column = pl.multiple_of((((1 - side) * KVD + h) * GROUP + p) * HD, HD)
                dq_ref[:, pl.ds(column, HD)] = dq_in[h, p * tok : (p + 1) * tok, :]
            x_copy(3, h).wait_recv()
            columns = pl.ds(pl.multiple_of(((1 - side) * KVD + h) * HD, HD), HD)
            dk_ref[:, columns] = dkv_in[h, 0]
            dv_ref[:, columns] = dkv_in[h, 1]
            for kind in range(4):
                x_copy(kind, h).wait_send()
            for s in range(UP):
                for way in (True, False):
                    if s < (UP if way else DOWN):
                        pl.when(ag_send_when(s, way))(
                            lambda s=s, way=way: ag_copy(h, s, way).wait_send()
                        )
                        pl.when(rs_send_when(s, way))(
                            lambda s=s, way=way: rs_copy(h, s, way).wait_send()
                        )
            return 0

        lax.fori_loop(0, KVD, collect, 0)
        for n in range(len(doubling)):
            count_copy(n).wait_send()

    steps = UP + DOWN
    rounds = t_bits + dp_bits
    dma = pltpu.SemaphoreType.DMA
    scratch = [
        pltpu.VMEM((KVD, 2, rows, HD), bf16),
        pltpu.VMEM((KVD, 2, length, HD), bf16),
        pltpu.VMEM((KVD, 2, rows2, HD), bf16),
        pltpu.VMEM((KVD, 2, tok, HD), bf16),
        pltpu.VMEM((length, rows), f32),
        pltpu.VMEM((length, rows), f32),
        pltpu.VMEM((length, rows), bf16),
        pltpu.VMEM((block, rows), bf16),
        pltpu.VMEM((HD, rows), f32),
        pltpu.VMEM((rows, HD), bf16),
        pltpu.VMEM((rows, HD), bf16),
        pltpu.VMEM((4, 8, rows), f32),
        pltpu.VMEM((8, rows), jnp.int32),
        pltpu.VMEM((2, 2, length, HD), f32),
        pltpu.VMEM((KVD, steps, 2, pair, HD), bf16),
        pltpu.VMEM((KVD, steps, 2, pair, HD), bf16),
        pltpu.VMEM((KVD, rows2, HD), bf16),
        pltpu.VMEM((KVD, rows2, HD), bf16),
        pltpu.VMEM((KVD, 2, tok, HD), bf16),
        pltpu.VMEM((KVD, 2, tok, HD), bf16),
        pltpu.VMEM((rounds + 1, 8, 128), f32),
        pltpu.VMEM((rounds, 8, 128), f32),
        dma((4, KVD)), dma((4, KVD)),
        dma((KVD, steps)), dma((KVD, steps)),
        dma((KVD, steps)), dma((KVD, steps)),
        dma((rounds,)), dma((rounds,)),
    ]
    return kernel, scratch


def body(queries, keys, values, out_grad, loss_mask):
    tok = queries.shape[1]
    ways = lax.axis_size("tensor")
    dp_size = lax.axis_size("dp")
    block = 256 if ways * tok % 256 == 0 else 2 * tok
    kernel, scratch = make_kernel(tok, dp_size, ways, block)
    vmem = pl.BlockSpec(memory_space=pltpu.VMEM)
    wide = jax.ShapeDtypeStruct((tok, queries.shape[2]), bf16)
    narrow = jax.ShapeDtypeStruct((tok, keys.shape[2]), bf16)
    query_grad, key_grad, value_grad = pl.pallas_call(
        kernel,
        out_shape=(wide, narrow, narrow),
        in_specs=[vmem] * 5,
        out_specs=(vmem, vmem, vmem),
        scratch_shapes=scratch,
        compiler_params=pltpu.CompilerParams(
            collective_id=0, has_side_effects=True, vmem_limit_bytes=62 * 2**20
        ),
    )(queries[0], keys[0], values[0], out_grad[0], loss_mask)
    return (query_grad[None], key_grad[None], value_grad[None])


def solution(mesh):
    return jax.shard_map(
        body,
        mesh=mesh,
        in_specs=(
            P("dp", "tensor", None),
            P("dp", "tensor", None),
            P("dp", "tensor", None),
            P("dp", "tensor", None),
            P("dp", "tensor"),
        ),
        out_specs=(P("dp", "tensor", None), P("dp", "tensor", None), P("dp", "tensor", None)),
        check_vma=False,
    )
```

```python
import jax
import jax.numpy as jnp
from jax import lax
from jax.experimental import pallas as pl
from jax.experimental.pallas import tpu as pltpu
from jax.sharding import PartitionSpec as P

HD = 128
KVH = 8
GROUP = 6
KVD = KVH // 2
RING = 8
UP = 4
DOWN = 3
SCALE = HD**-0.5
SCALE2 = SCALE * 1.4426950408889634
NT = (((1,), (1,)), ((), ()))
PARTS = 3
MESH = pl.DeviceIdType.MESH
f32 = jnp.float32
bf16 = jnp.bfloat16


def fold8(x):
    return x.reshape(x.shape[0] // 8, 8, x.shape[1])


def make_kernel(tok, dp_size, ways, block):
    rows2 = GROUP * tok
    rows = 2 * rows2
    pair = 2 * tok
    length = ways * tok
    blocks = length // block
    chunks = [(i, min(256, rows - i)) for i in range(0, rows, 256)]

    def digits(size):
        found, low = [], 1
        while low < size:
            found.append((low, min(4, size // low)))
            low *= found[-1][1]
        return found

    t_digits, dp_digits = digits(ways), digits(dp_size)

    def kernel(
        q_ref, k_ref, v_ref, g_ref, mask_ref, dq_ref, dk_ref, dv_ref,
        qg, kv, qg_out, kv_out, pbuf, ebuf, dsb, key_cols, dqt, qn, gn, stat, scales, rowpos,
        part, rs_out, rs_in, dq_out, dq_in, dkv_out, dkv_in, cnt_out, cnt_in,
        x_send, x_recv, ag_send, ag_recv, rs_send, rs_recv, cnt_send, cnt_recv,
    ):
        me_dp = lax.axis_index("dp")
        me = lax.axis_index("tensor")
        side = lax.rem(me, 2)
        y = me // 2

        def flips(index, low, size):
            digit = lax.rem(index // low, size)
            return [index + low * (lax.rem(digit + n, size) - digit) for n in range(1, size)]

        other = (me_dp, me + 1 - 2 * side)
        above = (me_dp, lax.rem(me + 2, ways))
        below = (me_dp, lax.rem(me + ways - 2, ways))
        rounds = [[(me_dp, t) for t in flips(me, low, size)] for low, size in t_digits] + [
            [(d, me) for d in flips(me_dp, low, size)] for low, size in dp_digits
        ]
        corner = me - lax.rem(me, 4) + 3 - lax.rem(me, 4)
        peers = [other, above, below, (me_dp, corner)]
        peers += [peer for group in rounds[1:] for peer in group]
        def clear(j, _):
            after = pl.ds(pl.multiple_of(j * pair, 16), pair)
            for h in range(KVD):
                kv[h, :, after, :] = jnp.zeros((2, pair, HD), bf16)
            return 0

        lax.fori_loop(y + 1, RING, clear, 0)
        barrier = pltpu.get_barrier_semaphore()
        for peer in peers:
            pl.semaphore_signal(barrier, inc=1, device_id=peer, device_id_type=MESH)

        def remote(src, dst, send, recv, device):
            return pltpu.make_async_remote_copy(
                src_ref=src, dst_ref=dst, send_sem=send, recv_sem=recv,
                device_id=device, device_id_type=MESH,
            )

        mask_row = mask_ref[...].astype(f32)
        eye = lax.broadcasted_iota(jnp.int32, (tok, tok), 0) == lax.broadcasted_iota(
            jnp.int32, (tok, tok), 1
        )
        mask_col = jnp.sum(jnp.where(eye, mask_row, 0.0), axis=1, keepdims=True)
        mask_tile = jnp.broadcast_to(mask_col, (tok, HD)).astype(bf16)
        cnt_out[0] = jnp.full((8, 128), jnp.sum(mask_row, keepdims=True)[0:1, 0:1], f32)

        own_rows = pl.multiple_of(side * rows2, 16)
        own_tok = pl.multiple_of(y * pair + side * tok, 16)

        def stage(h, _):
            for p in range(GROUP):
                at = pl.ds(p * tok, tok)
                mine = pl.ds(pl.multiple_of(((side * KVD + h) * GROUP + p) * HD, HD), HD)
                theirs = pl.ds(pl.multiple_of((((1 - side) * KVD + h) * GROUP + p) * HD, HD), HD)
                keep = pl.ds(pl.multiple_of(own_rows + p * tok, 16), tok)
                qg[h, 0, keep, :] = q_ref[:, mine]
                qg[h, 1, keep, :] = g_ref[:, mine] * mask_tile
                qg_out[h, 0, at, :] = q_ref[:, theirs]
                qg_out[h, 1, at, :] = g_ref[:, theirs] * mask_tile
            mine = pl.ds(pl.multiple_of((side * KVD + h) * HD, HD), HD)
            theirs = pl.ds(pl.multiple_of(((1 - side) * KVD + h) * HD, HD), HD)
            kv[h, 0, pl.ds(own_tok, tok), :] = k_ref[:, mine]
            kv[h, 1, pl.ds(own_tok, tok), :] = v_ref[:, mine]
            kv_out[h, 0] = k_ref[:, theirs]
            kv_out[h, 1] = v_ref[:, theirs]
            return 0

        lax.fori_loop(0, KVD, stage, 0)

        def clear_ds(b, _):
            dsb[pl.ds(pl.multiple_of(b * block, 16), block), :] = jnp.zeros((block, rows), bf16)
            return 0

        lax.fori_loop(0, blocks, clear_ds, 0)
        index = lax.broadcasted_iota(jnp.int32, (8, rows), 1)
        place = index
        for step in range(1, 2 * GROUP):
            place = place - jnp.where(index >= step * tok, tok, 0)
        rowpos[...] = place + jnp.where(index >= rows2, tok, 0)

        pl.semaphore_wait(barrier, len(peers))

        def x_copy(kind, h):
            src, dst = {
                0: lambda: (kv_out.at[h], kv.at[h, :, pl.ds(own_tok, tok), :]),
                1: lambda: (qg_out.at[h], qg.at[h, :, pl.ds(own_rows, rows2), :]),
                2: lambda: (dq_out.at[h], dq_in.at[h]),
                3: lambda: (dkv_out.at[h], dkv_in.at[h]),
            }[kind]()
            return remote(src, dst, x_send.at[kind, h], x_recv.at[kind, h], other)

        def ag_copy(h, s, up, i):
            j = y - s if up else lax.rem(y + s, RING)
            span = pl.ds(pl.multiple_of(jnp.maximum(j, 0) * pair, 16), pair)
            place = kv.at[h, i, span, :]
            slot = s if up else UP + s
            return remote(
                place, place, ag_send.at[h, slot, i], ag_recv.at[h, slot, i],
                above if up else below,
            )

        def ag_send_when(s, up):
            if up:
                return jnp.logical_and(y < RING - 1, y >= s)
            return lax.rem(y + s, RING) < DOWN

        def ag_recv_when(s, up):
            if up:
                return y >= s + 1
            return lax.rem(y + 1 + s, RING) < DOWN

        def ag_event(h, s):
            if s == 0:
                x_copy(0, h).wait_recv()
            for i in range(2):
                for up in (True, False):
                    last = UP if up else DOWN
                    if 1 <= s <= last:
                        pl.when(ag_recv_when(s - 1, up))(
                            lambda up=up, i=i: ag_copy(h, s - 1, up, i).wait_recv()
                        )
                    if s < last:
                        pl.when(ag_send_when(s, up))(
                            lambda up=up, i=i: ag_copy(h, s, up, i).start()
                        )

        def rs_copy(h, s, down):
            slot = s if down else UP + s
            return remote(
                rs_out.at[h, slot], rs_in.at[h, slot], rs_send.at[h, slot], rs_recv.at[h, slot],
                below if down else above,
            )

        def rs_block(s, down):
            return y - UP + s if down else lax.rem(y + DOWN - s, RING)

        def rs_send_when(s, down):
            if down:
                return y >= UP - s
            return lax.rem(y + DOWN - s, RING) < DOWN

        def rs_recv_when(s, down):
            if down:
                return jnp.logical_and(y < RING - 1, y >= UP - 1 - s)
            return lax.rem(y + DOWN - 1 - s, RING) < DOWN

        def rs_take(h, s, down):
            pl.when(rs_recv_when(s, down))(lambda: rs_copy(h, s, down).wait_recv())

        def the_factor():
            return f32(dp_size * length) / cnt_out[len(rounds)][0:1, :]

        def part_block(h, i, j):
            span = pl.ds(pl.multiple_of(jnp.maximum(j, 0) * pair, 16), pair)
            return part[lax.rem(h, PARTS), i, span, :]

        def rs_start(h, s):
            for down in (True, False):
                if s >= (UP if down else DOWN):
                    continue
                if s > 0:
                    rs_take(h, s - 1, down)
                slot = s if down else UP + s
                j = rs_block(s, down)
                here = rs_send_when(s, down)
                if down:
                    cases = [(True, s > 0, jnp.logical_and(here, y < RING - 1))]
                else:
                    cases = [(True, s > 0, jnp.logical_and(here, y > j))]
                    if s > 0:
                        cases.append((False, True, jnp.logical_and(here, y <= j)))
                for mine, came, when in cases:

                    def fill(mine=mine, came=came, slot=slot, j=j, down=down):
                        for i in range(2):
                            if mine and came:
                                total = part_block(h, i, j) + rs_in[h, slot - 1, i].astype(f32)
                                rs_out[h, slot, i] = total.astype(bf16)
                            elif mine:
                                rs_out[h, slot, i] = part_block(h, i, j).astype(bf16)
                            else:
                                rs_out[h, slot, i] = rs_in[h, slot - 1, i]
                        rs_copy(h, s, down).start()

                    pl.when(when)(fill)

        def rs_end(h, s):
            @pl.when(y == RING - 1)
            def _():
                for i in range(2):
                    rs_out[h, s, i] = part_block(h, i, RING - 1 - UP + s).astype(bf16)
                rs_copy(h, s, True).start()

        def rs_finish(h):
            rs_take(h, UP - 1, True)
            rs_take(h, DOWN - 1, False)
            mine_at = pl.ds(own_tok, tok)
            theirs_at = pl.ds(pl.multiple_of(y * pair + (1 - side) * tok, 16), tok)
            mine_in = pl.ds(pl.multiple_of(side * tok, 16), tok)
            theirs_in = pl.ds(pl.multiple_of((1 - side) * tok, 16), tok)
            columns = pl.ds(pl.multiple_of((side * KVD + h) * HD, HD), HD)
            from_above = y < RING - 1
            from_below = y < DOWN

            def total(i, at, within, above_too, below_too):
                value = part[lax.rem(h, PARTS), i, at, :]
                if above_too:
                    value = value + rs_in[h, UP - 1, i, within, :].astype(f32)
                if below_too:
                    value = value + rs_in[h, UP + DOWN - 1, i, within, :].astype(f32)
                return (value * (the_factor() * (SCALE if i == 0 else 1.0))).astype(bf16)

            for above_too, below_too, when in (
                (True, True, from_below),
                (True, False, jnp.logical_and(from_above, jnp.logical_not(from_below))),
                (False, False, jnp.logical_not(from_above)),
            ):

                def fill(above_too=above_too, below_too=below_too):
                    for i, ref in ((0, dk_ref), (1, dv_ref)):
                        dkv_out[h, i] = total(i, theirs_at, theirs_in, above_too, below_too)
                        ref[:, columns] = total(i, mine_at, mine_in, above_too, below_too)

                pl.when(when)(fill)
            x_copy(3, h).start()

        def count_copies(n):
            return [
                remote(
                    cnt_out.at[n], cnt_in.at[n, i], cnt_send.at[n, i], cnt_recv.at[n, i], peer
                )
                for i, peer in enumerate(rounds[n])
            ]

        def count_point(n):
            if 0 < n <= len(rounds):
                total = cnt_out[n - 1]
                for i, copy in enumerate(count_copies(n - 1)):
                    copy.wait_recv()
                    total = total + cnt_in[n - 1, i]
                cnt_out[n] = total
            if n < len(rounds):
                for copy in count_copies(n):
                    copy.start()

        x_copy(0, 0).start()
        count_point(0)
        x_copy(1, 0).start()
        ag_event(0, 0)
        x_copy(0, 1).start()

        gathers = {
            (0, "A0"): [(0, 1)],
            (0, "A1"): [(0, 2)],
            (0, "A2"): [(0, 3), (1, 0)],
            (0, "A3"): [(0, 4)],
            (0, "C"): [(1, 1)],
            (0, "E"): [(1, 2), (2, 0)],
            (1, "A1"): [(1, 3)],
            (1, "A2"): [(2, 1)],
            (1, "A3"): [(1, 4)],
            (1, "C"): [(2, 2), (3, 0)],
            (1, "E"): [(2, 3), (3, 1)],
            (2, "A0"): [(2, 4)],
            (2, "A1"): [(3, 2)],
            (2, "C"): [(3, 3)],
            (2, "E"): [(3, 4)],
        }
        counts = {(0, "A0"): 1, (0, "A2"): 2, (0, "E"): 3, (1, "A0"): 4, (1, "A2"): 5}
        exchanges = {
            (0, "A1"): [(1, 1), (0, 2)],
            (0, "C"): [(1, 2), (0, 3)],
            (1, "A0"): [(1, 3)],
        }

        def beside(h, place):
            for n in range(KVD):
                todo = (n, place)
                if todo not in gathers and todo not in counts and todo not in exchanges:
                    continue

                @pl.when(h == n)
                def _():
                    for kind, head in exchanges.get(todo, []):
                        x_copy(kind, head).start()
                    for head, s in gathers.get(todo, []):
                        ag_event(head, s)
                    if todo in counts:
                        count_point(counts[todo])

            if place in ("A1", "A2", "A3"):
                pl.when(h > 0)(lambda: rs_end(h - 1, int(place[1])))
            if place == "A2":
                pl.when(h > 0)(lambda: rs_start(h - 1, 1))
                pl.when(h > 1)(lambda: rs_start(h - 2, 3))

        held = (pair * (y + 1) + block - 1) // block
        high = y // (RING - 2)
        odd = lax.rem(y, 2)
        tiles = [
            (held - 1, None),
            (high * (2 - 2 * odd), y >= RING - 2),
            (high * 2 * odd + (1 - high) * jnp.maximum(held - 2, 0), held >= 2),
            (high + (1 - high) * jnp.maximum(held - 3, 0), held >= 3),
        ]

        def finish_queries(h):
            dq_rows = jnp.transpose(dqt[...] * (the_factor()[:, 0:1] * SCALE)).astype(bf16)

            def hand_out(mine, theirs):
                dq_out[h] = theirs
                for p in range(GROUP):
                    column = pl.multiple_of(((side * KVD + h) * GROUP + p) * HD, HD)
                    dq_ref[:, pl.ds(column, HD)] = mine[p * tok : (p + 1) * tok]

            pl.when(side == 0)(lambda: hand_out(dq_rows[:rows2], dq_rows[rows2:]))
            pl.when(side == 1)(lambda: hand_out(dq_rows[rows2:], dq_rows[:rows2]))
            x_copy(2, h).start()

        def one_head(h, _):
            stat[0] = jnp.full((8, rows), -1e30, f32)
            stat[1] = jnp.zeros((8, rows), f32)
            stat[2] = jnp.zeros((8, rows), f32)
            def weights(masked):
                def step(b, _):
                    at = pl.ds(pl.multiple_of(b * block, 16), block)
                    key_block = kv[h, 0, at, :]
                    value_block = kv[h, 1, at, :]
                    for c0, cw in chunks:
                        cs = pl.ds(c0, cw)
                        s = lax.dot_general(
                            key_block, qg[h, 0, cs, :], NT, preferred_element_type=f32
                        )
                        p = lax.dot_general(
                            value_block, qg[h, 1, cs, :], NT, preferred_element_type=f32
                        )
                        s = s * SCALE2
                        if masked:
                            key_at = (
                                b * block - pair * y
                                + lax.broadcasted_iota(jnp.int32, (block, cw), 0)
                            )
                            s = jnp.where(key_at <= rowpos[0:1, cs], s, -1e30)
                        pbuf[at, cs] = p
                        top = jnp.max(jnp.max(fold8(s), axis=0), axis=0, keepdims=True)
                        old = stat[0, 0:1, cs]
                        new = jnp.maximum(old, jnp.ceil(top))
                        change = jnp.exp2(old - new)
                        e = jnp.exp2(s - new)
                        ebuf[at, cs] = e.astype(bf16)
                        stat[0, :, cs] = jnp.broadcast_to(new, (8, cw))
                        scales[b, :, cs] = jnp.broadcast_to(new, (8, cw))
                        stat[1, :, cs] = stat[1, :, cs] * change + jnp.sum(fold8(e), axis=0)
                        stat[2, :, cs] = stat[2, :, cs] * change + jnp.sum(fold8(e * p), axis=0)
                    return 0

                return step

            beside(h, "A0")
            x_copy(1, h).wait_recv()
            for n, (tile, when) in enumerate(tiles):
                if n == 0:
                    weights(True)(tile, 0)
                else:
                    beside(h, f"A{n}")
                    pl.when(when)(lambda tile=tile: (weights(False)(tile, 0), None)[1])
            beside(h, "C")
            pl.when(h > 0)(lambda: finish_queries(h - 1))
            key_cols[...] = jnp.transpose(kv[h, 0])
            inverse = 1.0 / jnp.sum(stat[1], axis=0, keepdims=True)
            delta = jnp.sum(stat[2], axis=0, keepdims=True) * inverse
            stat[3] = jnp.broadcast_to(delta, (8, rows))
            inverse_column = jnp.transpose(jnp.broadcast_to(inverse, (8, rows)))[:, 0:1]
            qn[...] = (qg[h, 0].astype(f32) * inverse_column).astype(bf16)
            gn[...] = (qg[h, 1].astype(f32) * inverse_column).astype(bf16)
            slot = lax.rem(h, PARTS)

            def grads(b, _):
                at = pl.ds(pl.multiple_of(b * block, 16), block)
                for c0, cw in chunks:
                    cs = pl.ds(c0, cw)
                    change = jnp.exp2(scales[b, 0:1, cs] - stat[0, 0:1, cs]).astype(bf16)
                    e = ebuf[at, cs] * change
                    ebuf[at, cs] = e
                    dsb[at, cs] = e * (pbuf[at, cs] - stat[3, 0:1, cs]).astype(bf16)
                part[slot, 1, at, :] = jnp.dot(
                    ebuf[at, :], gn[...], preferred_element_type=f32
                )
                part[slot, 0, at, :] = jnp.dot(
                    dsb[at, :], qn[...], preferred_element_type=f32
                )
                return 0

            lax.fori_loop(0, held, grads, 0)
            rs_end(h, 0)
            rs_start(h, 0)
            beside(h, "E")
            for c0, cw in chunks:
                cs = pl.ds(c0, cw)
                dqt[:, cs] = inverse[:, c0 : c0 + cw] * jnp.dot(
                    key_cols[...], dsb[:, cs], preferred_element_type=f32
                )
            pl.when(h > 0)(lambda: rs_start(h - 1, 2))
            pl.when(h > 1)(lambda: rs_finish(h - 2))
            return 0

        lax.fori_loop(0, KVD, one_head, 0)
        last = KVD - 1

        @pl.when(y == RING - 1)
        def _():
            for s in range(1, UP):
                rs_copy(last, s - 1, True).wait_send()
                rs_end(last, s)

        finish_queries(last)

        def take_queries(h):
            x_copy(2, h).wait_recv()
            for p in range(GROUP):
                column = pl.multiple_of((((1 - side) * KVD + h) * GROUP + p) * HD, HD)
                dq_ref[:, pl.ds(column, HD)] = dq_in[h, p * tok : (p + 1) * tok, :]

        def settle(h, _):
            pl.when(h < last)(lambda: take_queries(h))
            for kind in range(3):
                x_copy(kind, h).wait_send()
            for s in range(UP):
                for way in (True, False):
                    if s < (UP if way else DOWN):
                        for i in range(2):
                            pl.when(ag_send_when(s, way))(
                                lambda s=s, way=way, i=i: ag_copy(h, s, way, i).wait_send()
                            )
            return 0

        def settle_sums(h, _):
            for s in range(UP):
                for way in (True, False):
                    if s < (UP if way else DOWN):
                        left = rs_send_when(s, way)
                        if way and s < UP - 1:
                            left = jnp.logical_and(left, jnp.logical_or(y < RING - 1, h < last))
                        pl.when(left)(lambda s=s, way=way: rs_copy(h, s, way).wait_send())
            return 0

        def take_sums(h, _):
            x_copy(3, h).wait_recv()
            columns = pl.ds(pl.multiple_of(((1 - side) * KVD + h) * HD, HD), HD)
            dk_ref[:, columns] = dkv_in[h, 0]
            dv_ref[:, columns] = dkv_in[h, 1]
            x_copy(3, h).wait_send()
            return 0

        rs_start(last, 1)
        rs_start(last - 1, 3)
        lax.fori_loop(0, KVD, settle, 0)
        rs_start(last, 2)
        rs_finish(last - 1)
        lax.fori_loop(0, last, settle_sums, 0)
        rs_start(last, 3)
        take_queries(last)
        lax.fori_loop(0, last, take_sums, 0)
        rs_finish(last)
        settle_sums(last, 0)
        take_sums(last, 0)
        for n in range(len(rounds)):
            for copy in count_copies(n):
                copy.wait_send()

    steps = UP + DOWN
    rounds = len(t_digits) + len(dp_digits)
    dma = pltpu.SemaphoreType.DMA
    scratch = [
        pltpu.VMEM((KVD, 2, rows, HD), bf16),
        pltpu.VMEM((KVD, 2, length, HD), bf16),
        pltpu.VMEM((KVD, 2, rows2, HD), bf16),
        pltpu.VMEM((KVD, 2, tok, HD), bf16),
        pltpu.VMEM((length, rows), f32),
        pltpu.VMEM((length, rows), bf16),
        pltpu.VMEM((length, rows), bf16),
        pltpu.VMEM((HD, length), bf16),
        pltpu.VMEM((HD, rows), f32),
        pltpu.VMEM((rows, HD), bf16),
        pltpu.VMEM((rows, HD), bf16),
        pltpu.VMEM((4, 8, rows), f32),
        pltpu.VMEM((blocks, 8, rows), f32),
        pltpu.VMEM((8, rows), jnp.int32),
        pltpu.VMEM((PARTS, 2, length, HD), f32),
        pltpu.VMEM((KVD, steps, 2, pair, HD), bf16),
        pltpu.VMEM((KVD, steps, 2, pair, HD), bf16),
        pltpu.VMEM((KVD, rows2, HD), bf16),
        pltpu.VMEM((KVD, rows2, HD), bf16),
        pltpu.VMEM((KVD, 2, tok, HD), bf16),
        pltpu.VMEM((KVD, 2, tok, HD), bf16),
        pltpu.VMEM((rounds + 1, 8, 128), f32),
        pltpu.VMEM((rounds, 3, 8, 128), f32),
        dma((4, KVD)), dma((4, KVD)),
        dma((KVD, steps, 2)), dma((KVD, steps, 2)),
        dma((KVD, steps)), dma((KVD, steps)),
        dma((rounds, 3)), dma((rounds, 3)),
    ]
    return kernel, scratch


def body(queries, keys, values, out_grad, loss_mask):
    tok = queries.shape[1]
    ways = lax.axis_size("tensor")
    dp_size = lax.axis_size("dp")
    block = 4 * tok
    kernel, scratch = make_kernel(tok, dp_size, ways, block)
    vmem = pl.BlockSpec(memory_space=pltpu.VMEM)
    wide = jax.ShapeDtypeStruct((tok, queries.shape[2]), bf16)
    narrow = jax.ShapeDtypeStruct((tok, keys.shape[2]), bf16)
    query_grad, key_grad, value_grad = pl.pallas_call(
        kernel,
        out_shape=(wide, narrow, narrow),
        in_specs=[vmem] * 5,
        out_specs=(vmem, vmem, vmem),
        scratch_shapes=scratch,
        compiler_params=pltpu.CompilerParams(
            collective_id=0, has_side_effects=True, vmem_limit_bytes=62 * 2**20
        ),
    )(queries[0], keys[0], values[0], out_grad[0], loss_mask)
    return (query_grad[None], key_grad[None], value_grad[None])


def solution(mesh):
    return jax.shard_map(
        body,
        mesh=mesh,
        in_specs=(
            P("dp", "tensor", None),
            P("dp", "tensor", None),
            P("dp", "tensor", None),
            P("dp", "tensor", None),
            P("dp", "tensor"),
        ),
        out_specs=(P("dp", "tensor", None), P("dp", "tensor", None), P("dp", "tensor", None)),
        check_vma=False,
    )
```

```python
import jax
import jax.numpy as jnp
from jax import lax
from jax.experimental import pallas as pl
from jax.experimental.pallas import tpu as pltpu
from jax.sharding import PartitionSpec as P

HD = 128
KVH = 8
GROUP = 6
KVD = KVH // 2
RING = 8
UP = 4
DOWN = 3
SCALE = HD**-0.5
SCALE2 = SCALE * 1.4426950408889634
NT = (((1,), (1,)), ((), ()))
PARTS = 3
MESH = pl.DeviceIdType.MESH
f32 = jnp.float32
bf16 = jnp.bfloat16


def fold8(x):
    return x.reshape(x.shape[0] // 8, 8, x.shape[1])


def make_kernel(tok, dp_size, ways, block):
    rows2 = GROUP * tok
    rows = 2 * rows2
    pair = 2 * tok
    length = ways * tok
    blocks = length // block
    chunks = [(i, min(256, rows - i)) for i in range(0, rows, 256)]

    def digits(size):
        found, low = [], 1
        while low < size:
            found.append((low, min(4, size // low)))
            low *= found[-1][1]
        return found

    t_digits, dp_digits = digits(ways), digits(dp_size)

    def kernel(
        q_ref, k_ref, v_ref, g_ref, mask_ref, dq_ref, dk_ref, dv_ref,
        qg, kv, qg_out, kv_out, pbuf, ebuf, dsb, key_cols, dqt, qn, gn, stat, scales, rowpos,
        part, rs_out, rs_in, dq_out, dq_in, dkv_out, dkv_in, cnt_out, cnt_in,
        x_send, x_recv, ag_send, ag_recv, rs_send, rs_recv, cnt_send, cnt_recv,
    ):
        me_dp = lax.axis_index("dp")
        me = lax.axis_index("tensor")
        side = lax.rem(me, 2)
        y = me // 2

        def flips(index, low, size):
            digit = lax.rem(index // low, size)
            return [index + low * (lax.rem(digit + n, size) - digit) for n in range(1, size)]

        other = (me_dp, me + 1 - 2 * side)
        above = (me_dp, lax.rem(me + 2, ways))
        below = (me_dp, lax.rem(me + ways - 2, ways))
        rounds = [[(me_dp, t) for t in flips(me, low, size)] for low, size in t_digits] + [
            [(d, me) for d in flips(me_dp, low, size)] for low, size in dp_digits
        ]
        corner = me - lax.rem(me, 4) + 3 - lax.rem(me, 4)
        peers = [other, above, below, (me_dp, corner)]
        peers += [peer for group in rounds[1:] for peer in group]
        def clear(j, _):
            after = pl.ds(pl.multiple_of(j * pair, 16), pair)
            for h in range(KVD):
                kv[h, :, after, :] = jnp.zeros((2, pair, HD), bf16)
            return 0

        lax.fori_loop(y + 1, RING, clear, 0)
        barrier = pltpu.get_barrier_semaphore()
        for peer in peers:
            pl.semaphore_signal(barrier, inc=1, device_id=peer, device_id_type=MESH)

        def remote(src, dst, send, recv, device):
            return pltpu.make_async_remote_copy(
                src_ref=src, dst_ref=dst, send_sem=send, recv_sem=recv,
                device_id=device, device_id_type=MESH,
            )

        mask_row = mask_ref[...].astype(f32)
        eye = lax.broadcasted_iota(jnp.int32, (tok, tok), 0) == lax.broadcasted_iota(
            jnp.int32, (tok, tok), 1
        )
        mask_col = jnp.sum(jnp.where(eye, mask_row, 0.0), axis=1, keepdims=True)
        mask_tile = jnp.broadcast_to(mask_col, (tok, HD)).astype(bf16)
        cnt_out[0] = jnp.full((8, 128), jnp.sum(mask_row, keepdims=True)[0:1, 0:1], f32)

        own_rows = pl.multiple_of(side * rows2, 16)
        own_tok = pl.multiple_of(y * pair + side * tok, 16)

        def stage(h, _):
            for p in range(GROUP):
                at = pl.ds(p * tok, tok)
                mine = pl.ds(pl.multiple_of(((side * KVD + h) * GROUP + p) * HD, HD), HD)
                theirs = pl.ds(pl.multiple_of((((1 - side) * KVD + h) * GROUP + p) * HD, HD), HD)
                keep = pl.ds(pl.multiple_of(own_rows + p * tok, 16), tok)
                qg[h, 0, keep, :] = q_ref[:, mine]
                qg[h, 1, keep, :] = g_ref[:, mine] * mask_tile
                qg_out[h, 0, at, :] = q_ref[:, theirs]
                qg_out[h, 1, at, :] = g_ref[:, theirs] * mask_tile
            mine = pl.ds(pl.multiple_of((side * KVD + h) * HD, HD), HD)
            theirs = pl.ds(pl.multiple_of(((1 - side) * KVD + h) * HD, HD), HD)
            kv[h, 0, pl.ds(own_tok, tok), :] = k_ref[:, mine]
            kv[h, 1, pl.ds(own_tok, tok), :] = v_ref[:, mine]
            kv_out[h, 0] = k_ref[:, theirs]
            kv_out[h, 1] = v_ref[:, theirs]
            return 0

        lax.fori_loop(0, KVD, stage, 0)

        def clear_ds(b, _):
            dsb[pl.ds(pl.multiple_of(b * block, 16), block), :] = jnp.zeros((block, rows), bf16)
            return 0

        lax.fori_loop(0, blocks, clear_ds, 0)
        index = lax.broadcasted_iota(jnp.int32, (8, rows), 1)
        place = index
        for step in range(1, 2 * GROUP):
            place = place - jnp.where(index >= step * tok, tok, 0)
        rowpos[...] = place + jnp.where(index >= rows2, tok, 0)

        pl.semaphore_wait(barrier, len(peers))

        def x_copy(kind, h):
            src, dst = {
                0: lambda: (kv_out.at[h], kv.at[h, :, pl.ds(own_tok, tok), :]),
                1: lambda: (qg_out.at[h], qg.at[h, :, pl.ds(own_rows, rows2), :]),
                2: lambda: (dq_out.at[h], dq_in.at[h]),
                3: lambda: (dkv_out.at[h], dkv_in.at[h]),
            }[kind]()
            return remote(src, dst, x_send.at[kind, h], x_recv.at[kind, h], other)

        def ag_copy(h, s, up, i):
            j = y - s if up else lax.rem(y + s, RING)
            span = pl.ds(pl.multiple_of(jnp.maximum(j, 0) * pair, 16), pair)
            place = kv.at[h, i, span, :]
            slot = s if up else UP + s
            return remote(
                place, place, ag_send.at[h, slot, i], ag_recv.at[h, slot, i],
                above if up else below,
            )

        def ag_send_when(s, up):
            if up:
                return jnp.logical_and(y < RING - 1, y >= s)
            return lax.rem(y + s, RING) < DOWN

        def ag_recv_when(s, up):
            if up:
                return y >= s + 1
            return lax.rem(y + 1 + s, RING) < DOWN

        def ag_event(h, s):
            if s == 0:
                x_copy(0, h).wait_recv()
            for i in range(2):
                for up in (True, False):
                    last = UP if up else DOWN
                    if 1 <= s <= last:
                        pl.when(ag_recv_when(s - 1, up))(
                            lambda up=up, i=i: ag_copy(h, s - 1, up, i).wait_recv()
                        )
                    if s < last:
                        pl.when(ag_send_when(s, up))(
                            lambda up=up, i=i: ag_copy(h, s, up, i).start()
                        )

        def rs_copy(h, s, down):
            slot = s if down else UP + s
            return remote(
                rs_out.at[h, slot], rs_in.at[h, slot], rs_send.at[h, slot], rs_recv.at[h, slot],
                below if down else above,
            )

        def rs_block(s, down):
            return y - UP + s if down else lax.rem(y + DOWN - s, RING)

        def rs_send_when(s, down):
            if down:
                return y >= UP - s
            return lax.rem(y + DOWN - s, RING) < DOWN

        def rs_recv_when(s, down):
            if down:
                return jnp.logical_and(y < RING - 1, y >= UP - 1 - s)
            return lax.rem(y + DOWN - 1 - s, RING) < DOWN

        def rs_take(h, s, down):
            pl.when(rs_recv_when(s, down))(lambda: rs_copy(h, s, down).wait_recv())

        def the_factor():
            return f32(dp_size * length) / cnt_out[len(rounds)][0:1, :]

        def part_block(h, i, j):
            span = pl.ds(pl.multiple_of(jnp.maximum(j, 0) * pair, 16), pair)
            return part[lax.rem(h, PARTS), i, span, :]

        def rs_start(h, s):
            for down in (True, False):
                if s >= (UP if down else DOWN):
                    continue
                if s > 0:
                    rs_take(h, s - 1, down)
                slot = s if down else UP + s
                j = rs_block(s, down)
                here = rs_send_when(s, down)
                if down:
                    cases = [(True, s > 0, jnp.logical_and(here, y < RING - 1))]
                else:
                    cases = [(True, s > 0, jnp.logical_and(here, y > j))]
                    if s > 0:
                        cases.append((False, True, jnp.logical_and(here, y <= j)))
                for mine, came, when in cases:

                    def fill(mine=mine, came=came, slot=slot, j=j, down=down):
                        for i in range(2):
                            if mine and came:
                                total = part_block(h, i, j) + rs_in[h, slot - 1, i].astype(f32)
                                rs_out[h, slot, i] = total.astype(bf16)
                            elif mine:
                                rs_out[h, slot, i] = part_block(h, i, j).astype(bf16)
                            else:
                                rs_out[h, slot, i] = rs_in[h, slot - 1, i]
                        rs_copy(h, s, down).start()

                    pl.when(when)(fill)

        def rs_end(h, s):
            @pl.when(y == RING - 1)
            def _():
                for i in range(2):
                    rs_out[h, s, i] = part_block(h, i, RING - 1 - UP + s).astype(bf16)
                rs_copy(h, s, True).start()

        def rs_finish(h):
            rs_take(h, UP - 1, True)
            rs_take(h, DOWN - 1, False)
            mine_at = pl.ds(own_tok, tok)
            theirs_at = pl.ds(pl.multiple_of(y * pair + (1 - side) * tok, 16), tok)
            mine_in = pl.ds(pl.multiple_of(side * tok, 16), tok)
            theirs_in = pl.ds(pl.multiple_of((1 - side) * tok, 16), tok)
            columns = pl.ds(pl.multiple_of((side * KVD + h) * HD, HD), HD)
            from_above = y < RING - 1
            from_below = y < DOWN

            def total(i, at, within, above_too, below_too):
                value = part[lax.rem(h, PARTS), i, at, :]
                if above_too:
                    value = value + rs_in[h, UP - 1, i, within, :].astype(f32)
                if below_too:
                    value = value + rs_in[h, UP + DOWN - 1, i, within, :].astype(f32)
                return (value * (the_factor() * (SCALE if i == 0 else 1.0))).astype(bf16)

            for above_too, below_too, when in (
                (True, True, from_below),
                (True, False, jnp.logical_and(from_above, jnp.logical_not(from_below))),
                (False, False, jnp.logical_not(from_above)),
            ):

                def fill(above_too=above_too, below_too=below_too):
                    for i, ref in ((0, dk_ref), (1, dv_ref)):
                        dkv_out[h, i] = total(i, theirs_at, theirs_in, above_too, below_too)
                        ref[:, columns] = total(i, mine_at, mine_in, above_too, below_too)

                pl.when(when)(fill)
            x_copy(3, h).start()

        def count_copies(n):
            return [
                remote(
                    cnt_out.at[n], cnt_in.at[n, i], cnt_send.at[n, i], cnt_recv.at[n, i], peer
                )
                for i, peer in enumerate(rounds[n])
            ]

        def count_point(n):
            if 0 < n <= len(rounds):
                total = cnt_out[n - 1]
                for i, copy in enumerate(count_copies(n - 1)):
                    copy.wait_recv()
                    total = total + cnt_in[n - 1, i]
                cnt_out[n] = total
            if n < len(rounds):
                for copy in count_copies(n):
                    copy.start()

        x_copy(0, 0).start()
        count_point(0)
        ag_event(0, 0)
        x_copy(1, 0).start()
        x_copy(0, 1).start()

        gathers = {
            (0, "A0"): [(0, 1)],
            (0, "A1"): [(0, 2)],
            (0, "A2"): [(0, 3), (1, 0)],
            (0, "A3"): [(0, 4)],
            (0, "C"): [(1, 1)],
            (0, "E"): [(1, 2), (2, 0)],
            (1, "A1"): [(1, 3)],
            (1, "A2"): [(2, 1)],
            (1, "A3"): [(1, 4)],
            (1, "C"): [(2, 2), (3, 0)],
            (1, "E"): [(2, 3), (3, 1)],
            (2, "A0"): [(2, 4)],
            (2, "A1"): [(3, 2)],
            (2, "C"): [(3, 3)],
            (2, "E"): [(3, 4)],
        }
        counts = {(0, "A0"): 1, (0, "A2"): 2, (0, "E"): 3, (1, "A0"): 4, (1, "A2"): 5}
        exchanges = {
            (0, "A1"): [(1, 1), (0, 2)],
            (0, "C"): [(1, 2), (0, 3)],
            (1, "A0"): [(1, 3)],
        }

        def beside(h, place):
            for n in range(KVD):
                todo = (n, place)
                if todo not in gathers and todo not in counts and todo not in exchanges:
                    continue

                @pl.when(h == n)
                def _():
                    for kind, head in exchanges.get(todo, []):
                        x_copy(kind, head).start()
                    for head, s in gathers.get(todo, []):
                        ag_event(head, s)
                    if todo in counts:
                        count_point(counts[todo])

            if place in ("A1", "A2", "A3"):
                pl.when(h > 0)(lambda: rs_end(h - 1, int(place[1])))
            if place == "A2":
                pl.when(h > 0)(lambda: rs_start(h - 1, 1))
                pl.when(h > 1)(lambda: rs_start(h - 2, 3))

        held = (pair * (y + 1) + block - 1) // block
        high = y // (RING - 2)
        odd = lax.rem(y, 2)
        tiles = [
            (held - 1, None),
            (high * (2 - 2 * odd), y >= RING - 2),
            (high * 2 * odd + (1 - high) * jnp.maximum(held - 2, 0), held >= 2),
            (high + (1 - high) * jnp.maximum(held - 3, 0), held >= 3),
        ]

        def finish_queries(h):
            dq_rows = jnp.transpose((dqt[...] * (the_factor()[:, 0:1] * SCALE)).astype(bf16))

            def hand_out(mine, theirs):
                dq_out[h] = theirs
                for p in range(GROUP):
                    column = pl.multiple_of(((side * KVD + h) * GROUP + p) * HD, HD)
                    dq_ref[:, pl.ds(column, HD)] = mine[p * tok : (p + 1) * tok]

            pl.when(side == 0)(lambda: hand_out(dq_rows[:rows2], dq_rows[rows2:]))
            pl.when(side == 1)(lambda: hand_out(dq_rows[rows2:], dq_rows[:rows2]))
            x_copy(2, h).start()

        def one_head(h, _):
            stat[0] = jnp.full((8, rows), -1e30, f32)
            stat[1] = jnp.zeros((8, rows), f32)
            stat[2] = jnp.zeros((8, rows), f32)
            def weights(masked):
                def step(b, _):
                    at = pl.ds(pl.multiple_of(b * block, 16), block)
                    key_block = kv[h, 0, at, :]
                    value_block = kv[h, 1, at, :]
                    for c0, cw in chunks:
                        cs = pl.ds(c0, cw)
                        s = lax.dot_general(
                            key_block, qg[h, 0, cs, :], NT, preferred_element_type=f32
                        )
                        p = lax.dot_general(
                            value_block, qg[h, 1, cs, :], NT, preferred_element_type=f32
                        )
                        s = s * SCALE2
                        if masked:
                            key_at = (
                                b * block - pair * y
                                + lax.broadcasted_iota(jnp.int32, (block, cw), 0)
                            )
                            s = jnp.where(key_at <= rowpos[0:1, cs], s, -1e30)
                        pbuf[at, cs] = p
                        top = jnp.max(jnp.max(fold8(s), axis=0), axis=0, keepdims=True)
                        old = stat[0, 0:1, cs]
                        new = jnp.maximum(old, jnp.ceil(top))
                        change = jnp.exp2(old - new)
                        e = jnp.exp2(s - new)
                        ebuf[at, cs] = e.astype(bf16)
                        stat[0, :, cs] = jnp.broadcast_to(new, (8, cw))
                        scales[b, :, cs] = jnp.broadcast_to(new, (8, cw))
                        stat[1, :, cs] = stat[1, :, cs] * change + jnp.sum(fold8(e), axis=0)
                        stat[2, :, cs] = stat[2, :, cs] * change + jnp.sum(fold8(e * p), axis=0)
                    return 0

                return step

            beside(h, "A0")
            x_copy(1, h).wait_recv()
            for n, (tile, when) in enumerate(tiles):
                if n == 0:
                    weights(True)(tile, 0)
                else:
                    beside(h, f"A{n}")
                    pl.when(when)(lambda tile=tile: (weights(False)(tile, 0), None)[1])
            beside(h, "C")
            pl.when(h > 0)(lambda: finish_queries(h - 1))
            key_cols[...] = jnp.transpose(kv[h, 0])
            inverse = 1.0 / jnp.sum(stat[1], axis=0, keepdims=True)
            delta = jnp.sum(stat[2], axis=0, keepdims=True) * inverse
            stat[3] = jnp.broadcast_to(delta, (8, rows))
            inverse_column = jnp.transpose(jnp.broadcast_to(inverse, (8, rows)))[:, 0:1]
            qn[...] = (qg[h, 0].astype(f32) * inverse_column).astype(bf16)
            gn[...] = (qg[h, 1].astype(f32) * inverse_column).astype(bf16)
            slot = lax.rem(h, PARTS)

            def grads(b, _):
                at = pl.ds(pl.multiple_of(b * block, 16), block)
                for c0, cw in chunks:
                    cs = pl.ds(c0, cw)
                    change = jnp.exp2(scales[b, 0:1, cs] - stat[0, 0:1, cs]).astype(bf16)
                    e = ebuf[at, cs] * change
                    ebuf[at, cs] = e
                    dsb[at, cs] = e * (pbuf[at, cs] - stat[3, 0:1, cs]).astype(bf16)
                part[slot, 1, at, :] = jnp.dot(
                    ebuf[at, :], gn[...], preferred_element_type=f32
                )
                part[slot, 0, at, :] = jnp.dot(
                    dsb[at, :], qn[...], preferred_element_type=f32
                )
                return 0

            lax.fori_loop(0, held, grads, 0)
            rs_end(h, 0)
            rs_start(h, 0)
            beside(h, "E")
            for c0, cw in chunks:
                cs = pl.ds(c0, cw)
                dqt[:, cs] = inverse[:, c0 : c0 + cw] * jnp.dot(
                    key_cols[...], dsb[:, cs], preferred_element_type=f32
                )
            pl.when(h > 0)(lambda: rs_start(h - 1, 2))
            pl.when(h > 1)(lambda: rs_finish(h - 2))
            return 0

        lax.fori_loop(0, KVD, one_head, 0)
        last = KVD - 1

        @pl.when(y == RING - 1)
        def _():
            for s in range(1, UP):
                rs_copy(last, s - 1, True).wait_send()
                rs_end(last, s)

        finish_queries(last)

        def take_queries(h):
            x_copy(2, h).wait_recv()
            for p in range(GROUP):
                column = pl.multiple_of((((1 - side) * KVD + h) * GROUP + p) * HD, HD)
                dq_ref[:, pl.ds(column, HD)] = dq_in[h, p * tok : (p + 1) * tok, :]

        def settle(h, _):
            pl.when(h < last)(lambda: take_queries(h))
            for kind in range(3):
                x_copy(kind, h).wait_send()
            for s in range(UP):
                for way in (True, False):
                    if s < (UP if way else DOWN):
                        for i in range(2):
                            pl.when(ag_send_when(s, way))(
                                lambda s=s, way=way, i=i: ag_copy(h, s, way, i).wait_send()
                            )
            return 0

        def settle_sums(h, _):
            for s in range(UP):
                for way in (True, False):
                    if s < (UP if way else DOWN):
                        left = rs_send_when(s, way)
                        if way and s < UP - 1:
                            left = jnp.logical_and(left, jnp.logical_or(y < RING - 1, h < last))
                        pl.when(left)(lambda s=s, way=way: rs_copy(h, s, way).wait_send())
            return 0

        def take_sums(h, _):
            x_copy(3, h).wait_recv()
            columns = pl.ds(pl.multiple_of(((1 - side) * KVD + h) * HD, HD), HD)
            dk_ref[:, columns] = dkv_in[h, 0]
            dv_ref[:, columns] = dkv_in[h, 1]
            x_copy(3, h).wait_send()
            return 0

        rs_start(last, 1)
        rs_start(last - 1, 3)
        lax.fori_loop(0, KVD, settle, 0)
        rs_start(last, 2)
        rs_finish(last - 1)
        lax.fori_loop(0, last, settle_sums, 0)
        rs_start(last, 3)
        take_queries(last)
        lax.fori_loop(0, last, take_sums, 0)
        rs_finish(last)
        settle_sums(last, 0)
        take_sums(last, 0)
        for n in range(len(rounds)):
            for copy in count_copies(n):
                copy.wait_send()

    steps = UP + DOWN
    rounds = len(t_digits) + len(dp_digits)
    dma = pltpu.SemaphoreType.DMA
    scratch = [
        pltpu.VMEM((KVD, 2, rows, HD), bf16),
        pltpu.VMEM((KVD, 2, length, HD), bf16),
        pltpu.VMEM((KVD, 2, rows2, HD), bf16),
        pltpu.VMEM((KVD, 2, tok, HD), bf16),
        pltpu.VMEM((length, rows), f32),
        pltpu.VMEM((length, rows), bf16),
        pltpu.VMEM((length, rows), bf16),
        pltpu.VMEM((HD, length), bf16),
        pltpu.VMEM((HD, rows), f32),
        pltpu.VMEM((rows, HD), bf16),
        pltpu.VMEM((rows, HD), bf16),
        pltpu.VMEM((4, 8, rows), f32),
        pltpu.VMEM((blocks, 8, rows), f32),
        pltpu.VMEM((8, rows), jnp.int32),
        pltpu.VMEM((PARTS, 2, length, HD), f32),
        pltpu.VMEM((KVD, steps, 2, pair, HD), bf16),
        pltpu.VMEM((KVD, steps, 2, pair, HD), bf16),
        pltpu.VMEM((KVD, rows2, HD), bf16),
        pltpu.VMEM((KVD, rows2, HD), bf16),
        pltpu.VMEM((KVD, 2, tok, HD), bf16),
        pltpu.VMEM((KVD, 2, tok, HD), bf16),
        pltpu.VMEM((rounds + 1, 8, 128), f32),
        pltpu.VMEM((rounds, 3, 8, 128), f32),
        dma((4, KVD)), dma((4, KVD)),
        dma((KVD, steps, 2)), dma((KVD, steps, 2)),
        dma((KVD, steps)), dma((KVD, steps)),
        dma((rounds, 3)), dma((rounds, 3)),
    ]
    return kernel, scratch


def body(queries, keys, values, out_grad, loss_mask):
    tok = queries.shape[1]
    ways = lax.axis_size("tensor")
    dp_size = lax.axis_size("dp")
    block = 4 * tok
    kernel, scratch = make_kernel(tok, dp_size, ways, block)
    vmem = pl.BlockSpec(memory_space=pltpu.VMEM)
    wide = jax.ShapeDtypeStruct((tok, queries.shape[2]), bf16)
    narrow = jax.ShapeDtypeStruct((tok, keys.shape[2]), bf16)
    query_grad, key_grad, value_grad = pl.pallas_call(
        kernel,
        out_shape=(wide, narrow, narrow),
        in_specs=[vmem] * 5,
        out_specs=(vmem, vmem, vmem),
        scratch_shapes=scratch,
        compiler_params=pltpu.CompilerParams(
            collective_id=0, has_side_effects=True, vmem_limit_bytes=62 * 2**20
        ),
    )(queries[0], keys[0], values[0], out_grad[0], loss_mask)
    return (query_grad[None], key_grad[None], value_grad[None])


def solution(mesh):
    return jax.shard_map(
        body,
        mesh=mesh,
        in_specs=(
            P("dp", "tensor", None),
            P("dp", "tensor", None),
            P("dp", "tensor", None),
            P("dp", "tensor", None),
            P("dp", "tensor"),
        ),
        out_specs=(P("dp", "tensor", None), P("dp", "tensor", None), P("dp", "tensor", None)),
        check_vma=False,
    )
```
